256 devices in a mesh: island: 8 (over z_hi, x), fsdp: 32 (over z_lo, y, core).
Axes of the slice: x: 4, y: 4, z: 8 (z_hi: 2, z_lo: 4; z = z_hi * 4 + z_lo), core: 2. Of those that a mesh axis runs over, the one named last changes fastest.
Arguments:
- normed: bfloat16 [8, 8192, 8192], P('island', 'fsdp'), may hold values from -6 to 6
- cotangent: bfloat16 [8, 8192, 512], P('island', 'fsdp'), may hold values from -6 to 6
- weights: float32 [8, 8192, 512], P('island', 'fsdp'), may hold values from -6 to 6
- first_moment: float32 [8, 8192, 512], P('island', 'fsdp'), may hold values from -6 to 6
- second_moment: float32 [8, 8192, 512], P('island', 'fsdp'), may hold values from 0.05 to 2
- outer_params: float32 [8192, 128], P(('fsdp', 'island')), may hold values from -6 to 6
- outer_momentum: float32 [8192, 128], P(('fsdp', 'island')), may hold values from -6 to 6
- fragment: int32 [1], replicated, may hold values from 0 to 384
Outputs:
- grad_input: bfloat16 [8, 8192, 8192], P('island', 'fsdp')
- new_weights: float32 [8, 8192, 512], P('island', 'fsdp')
- new_first: float32 [8, 8192, 512], P('island', 'fsdp')
- new_second: float32 [8, 8192, 512], P('island', 'fsdp')
- new_outer: float32 [8192, 128], P(('fsdp', 'island'))
- new_momentum: float32 [8192, 128], P(('fsdp', 'island'))
The draws below stay inside these ranges and needn't reach their ends.
All inputs are finite; a program needn't handle non-finite values.
Results may differ from the reference program's by a relative error of at most 0.012.
Values may be sent and summed in bfloat16 or wider, within the bound.
No kernel may reach another device: no remote copies, remote signals or barrier semaphores. Data moves between devices by JAX's collectives and lax.ppermute only.
A program may use at most 128 MiB of HBM per device.

```python
import math
import jax
import jax.numpy as jnp
from jax import lax

D = 8192
HEAD = 128
KVW = 512
TOK_ISL = 8192
ISLANDS = 8


def strengthened(values, stream_key, source, target, parts, factor):
    owner, partner = [(jnp.arange(values.shape[axis_at]) // (values.shape[axis_at] // parts)).reshape([-1 if axis == axis_at else 1 for axis in range(values.ndim)]) for axis_at in (source, target)]
    chosen = jax.random.permutation(stream_key, parts)[partner]
    strong = (owner == chosen) | (owner == (partner + parts // 2) % parts)
    return jnp.where(strong, factor * values, values)


def shard_levels(key, dims, pieces, smallest, top_value):
    level = 1.0
    for axis_at, shards_of in pieces:
        draws = jax.random.uniform(jax.random.fold_in(jax.random.fold_in(key, 6), axis_at), (shards_of,), jnp.float32, smallest / len(pieces), top_value / len(pieces))
        level = level * jnp.repeat(jnp.exp(draws), dims[axis_at] // shards_of).reshape((-1,) + (1,) * (len(dims) - 1 - axis_at))
    return level


def gaussian(key, extent, deviation, reach, cuts=(), held_as=jnp.bfloat16):
    factor_of = shard_levels(key, extent, cuts, -0.22, 0.18) if cuts else 1.0
    array = jax.random.normal(key, extent, jnp.float32) * deviation * factor_of
    return jnp.minimum(jnp.maximum(array, -reach), reach).astype(held_as)


def heavy_noise(own_key, dims, scale, reach, pieces, heavy, dtype=jnp.bfloat16):
    entries = scale * jax.random.normal(own_key, dims, jnp.float32)
    if pieces:
        entries = entries * shard_levels(own_key, dims, pieces, -0.22, 0.18)
    return jnp.clip(strengthened(entries, jax.random.fold_in(own_key, 3), *heavy), -reach, reach).astype(dtype)


def setup_inputs(seed: int = 0) -> dict:
    splits = jax.random.split(jax.random.key(seed), 9)
    normed = heavy_noise(splits[0], (ISLANDS, TOK_ISL, D), 1.0, 6.0, ((0, 8), (1, 32)), (1, 2, 32, 2.75))
    cotangent = gaussian(splits[1], (ISLANDS, TOK_ISL, KVW), 1.0, 6.0, ((0, 8), (1, 32)))
    weights = gaussian(splits[2], (ISLANDS, D, KVW), 1.0, 6.0, ((0, 8), (1, 32)), jnp.float32)
    first_moment = gaussian(splits[3], (ISLANDS, D, KVW), 1.0, 6.0, ((0, 8), (1, 32)), jnp.float32)
    second_moment = jnp.clip(jnp.exp(math.log(2.0) - 3.6888794 * jax.random.uniform(splits[4], (ISLANDS, D, KVW), jnp.float32) ** shard_levels(splits[4], (ISLANDS, D, KVW), ((0, 8), (1, 32)), -0.2, 0.2)), 0.05, 2.0)
    outer_params = gaussian(splits[5], (D, HEAD), 1.0, 6.0, ((0, 256),), jnp.float32)
    outer_momentum = gaussian(splits[6], (D, HEAD), 1.0, 6.0, ((0, 256),), jnp.float32)
    fragment = jax.random.randint(splits[7], (1,), 0, KVW - HEAD + 1).astype(jnp.int32)
    return {"normed": normed, "cotangent": cotangent, "weights": weights, "first_moment": first_moment, "second_moment": second_moment, "outer_params": outer_params, "outer_momentum": outer_momentum, "fragment": fragment}


BETA_FIRST = 0.9
BETA_SECOND = 0.95
EPSILON = 1e-08
INNER_RATE = 0.01
DECAY_RATE = 0.1
OUTER_RATE = 0.7
MOMENTUM = 0.9
MIX_WEIGHT = 0.5

def island_terms(operands):
    tokens_in, cotan, w_half = operands
    factor = 1.0 / math.sqrt(tokens_in.shape[1])
    back_grad = lax.dot_general(cotan, w_half, (((1,), (1,)), ((), ())), preferred_element_type=jnp.float32) * factor
    gradient = lax.dot_general(tokens_in, cotan, (((0,), (0,)), ((), ())), preferred_element_type=jnp.float32) * factor
    return (back_grad.astype(jnp.bfloat16), gradient)

def reference(normed, cotangent, weights, first_moment, second_moment, outer_params, outer_momentum, fragment):
    w_half = weights.astype(jnp.bfloat16)
    grad_input, gradient = lax.map(island_terms, (normed, cotangent, w_half))
    new_first = BETA_FIRST * first_moment + (1.0 - BETA_FIRST) * gradient
    new_second = BETA_SECOND * second_moment + (1.0 - BETA_SECOND) * gradient * gradient
    stepped = weights - INNER_RATE * (new_first / (jnp.sqrt(new_second) + EPSILON) + DECAY_RATE * weights)
    head_width = outer_params.shape[1]
    offset = fragment[0].astype(jnp.int32)
    inner_frag = lax.dynamic_slice_in_dim(weights, offset, head_width, 2)
    pseudo_grad = outer_params - lax.optimization_barrier(jnp.sum(inner_frag, axis=0)) / weights.shape[0]
    new_momentum = MOMENTUM * outer_momentum + pseudo_grad
    new_outer = outer_params - OUTER_RATE * (pseudo_grad + MOMENTUM * new_momentum)
    blended = MIX_WEIGHT * lax.dynamic_slice_in_dim(stepped, offset, head_width, 2) + (1.0 - MIX_WEIGHT) * new_outer[None]
    new_weights = lax.dynamic_update_slice_in_dim(stepped, blended, offset, 2)
    return (grad_input, new_weights, new_first, new_second, new_outer, new_momentum)
```

```python
import math

import jax
import jax.numpy as jnp
from jax import lax
from jax.experimental import pallas as pl
from jax.experimental.pallas import tpu as pltpu
from jax.sharding import PartitionSpec as P

BETA_FIRST = 0.9
BETA_SECOND = 0.95
EPSILON = 1e-08
INNER_RATE = 0.01
DECAY_RATE = 0.1
OUTER_RATE = 0.7
MOMENTUM = 0.9
MIX_WEIGHT = 0.5

NZ, NY, NC = 4, 4, 2
NX = 4
F32, BF16 = jnp.float32, jnp.bfloat16
COST = pl.CostEstimate(flops=1, bytes_accessed=1, transcendentals=0)
VMEM_LIMIT = 8 * 1024 * 1024

SMEM_SPEC = pl.BlockSpec(memory_space=pltpu.SMEM)
VMEM_SPEC = pl.BlockSpec(memory_space=pltpu.VMEM)
ANY_SPEC = pl.BlockSpec(memory_space=pl.ANY)


def fsdp_perm(move):
    pairs = []
    for z in range(NZ):
        for y in range(NY):
            for c in range(NC):
                tz, ty, tc = move(z, y, c)
                pairs.append(((z * NY + y) * NC + c, ((tz % NZ) * NY + ty % NY) * NC + tc))
    return pairs


def turned_perms(move):
    return [fsdp_perm(lambda z, y, c, k=k: move(z, y, c, k if c == 0 else -k)) for k in (1, -1)]


ON_Y, BACK_Y = turned_perms(lambda z, y, c, k: (z, y + k, c))
ON_Z, BACK_Z = turned_perms(lambda z, y, c, k: (z + k, y, c))
SWAP = fsdp_perm(lambda z, y, c: (z, y, 1 - c))


def island_perm(move):
    pairs = []
    for h in range(2):
        for x in range(NX):
            th, tx = move(h, x)
            pairs.append((h * NX + x, th * NX + tx))
    return pairs


PAIR_X = island_perm(lambda h, x: (h, x ^ 1))
CROSS_X = island_perm(lambda h, x: (h, 3 - x))
SWAP_H = island_perm(lambda h, x: (1 - h, x))


def params():
    return pltpu.CompilerParams(vmem_limit_bytes=VMEM_LIMIT)


def halve(master):
    def body(master, out):
        out[...] = master[...].astype(BF16)

    return pl.pallas_call(
        body,
        out_shape=jax.ShapeDtypeStruct(master.shape, BF16),
        in_specs=[VMEM_SPEC],
        out_specs=VMEM_SPEC,
        compiler_params=params(),
        cost_estimate=COST,
    )(master)


def pack(table, groups, normed, cotan, rows):
    tokens, kvw = cotan.shape
    halves = kvw // rows
    extra = [halves] + [0] * (len(groups) - 2) + [halves]

    def body(table, normed, cotan, *outs):
        for h in range(halves):
            turned = cotan[:, h * rows : (h + 1) * rows].T
            for i in (0, len(groups) - 1):
                outs[i][len(groups[i]) + h] = turned
        for out, places in zip(outs, groups):
            for j, place in enumerate(places):
                cols = pl.ds(pl.multiple_of(table[place] * rows, rows), rows)
                out[j] = normed[:, cols]

    return pl.pallas_call(
        body,
        out_shape=[
            jax.ShapeDtypeStruct((len(g) + n, tokens, rows), BF16) for g, n in zip(groups, extra)
        ],
        in_specs=[SMEM_SPEC] + [VMEM_SPEC] * 2,
        out_specs=[VMEM_SPEC] * len(groups),
        compiler_params=params(),
        cost_estimate=COST,
    )(table, normed, cotan)


def join(pieces):
    def body(*refs):
        at = 0
        for ref in refs[:-1]:
            refs[-1][pl.ds(at, ref.shape[0]), :] = ref[...]
            at += ref.shape[0]

    rows, columns = pieces[0].shape
    return pl.pallas_call(
        body,
        out_shape=jax.ShapeDtypeStruct((len(pieces) * rows, columns), pieces[0].dtype),
        in_specs=[VMEM_SPEC] * len(pieces),
        out_specs=VMEM_SPEC,
        compiler_params=params(),
        cost_estimate=COST,
    )(*pieces)


def grad_blocks(first, packed_first, groups, factor, own, swapped, packed):
    width = own.shape[2]
    halves = 2

    def body(own, swapped, packed, *outs):
        for group, out in enumerate(outs):
            for j in range(NZ):
                at = group * NZ + j
                for half in range(halves):
                    mine, theirs = own.shape[0] - halves + half, swapped.shape[0] - halves + half
                    total = jnp.dot(own[mine], own[first + at], preferred_element_type=F32)
                    total += jnp.dot(
                        swapped[theirs], packed[packed_first + at], preferred_element_type=F32
                    )
                    out[j, pl.ds(half * width, width), :] = (total * factor).astype(BF16)

    return pl.pallas_call(
        body,
        out_shape=[jax.ShapeDtypeStruct((NZ, halves * width, width), BF16)] * groups,
        in_specs=[VMEM_SPEC] * 3,
        out_specs=[VMEM_SPEC] * groups,
        compiler_params=params(),
        cost_estimate=COST,
    )(own, swapped, packed)


def add(*parts, split=False):
    blocks, *block = parts[0].shape

    def body(*refs):
        ins, outs = refs[: len(parts)], refs[len(parts) :]
        for j in range(blocks):
            total = ins[0][j].astype(F32)
            for ref in ins[1:]:
                total += ref[j].astype(F32)
            if split:
                outs[j][...] = total.astype(BF16)
            else:
                outs[0][j] = total.astype(BF16)

    shapes = [block] * blocks if split else [parts[0].shape]
    return pl.pallas_call(
        body,
        out_shape=[jax.ShapeDtypeStruct(tuple(shape), BF16) for shape in shapes],
        in_specs=[VMEM_SPEC] * len(parts),
        out_specs=[VMEM_SPEC] * len(shapes),
        compiler_params=params(),
        cost_estimate=COST,
    )(*parts)


def add_one(a, b):
    def body(a, b, out):
        out[...] = (a[...].astype(F32) + b[...].astype(F32)).astype(BF16)

    return pl.pallas_call(
        body,
        out_shape=jax.ShapeDtypeStruct(a.shape, BF16),
        in_specs=[VMEM_SPEC] * 2,
        out_specs=VMEM_SPEC,
        compiler_params=params(),
        cost_estimate=COST,
    )(a, b)


def input_blocks(table, entries, cotan, pieces, width, factor, dest=None):
    rows = width // (NZ * NY * NC)
    total = len(entries)
    operands = [table, cotan, *pieces]
    specs = [SMEM_SPEC] + [VMEM_SPEC] * (1 + len(pieces))
    aliases = {}
    if dest is not None:
        aliases = {len(operands): 0}
        operands.append(dest)
        specs.append(ANY_SPEC)

    def body(table, cotan, *refs):
        out, stage, sems = refs[-3:]
        copies = []
        for piece in refs[: len(pieces)]:
            for b in range(piece.shape[0] // rows):
                j = len(copies)
                block = piece[pl.ds(b * rows, rows), :]
                res = lax.dot_general(
                    cotan[...], block, (((1,), (1,)), ((), ())), preferred_element_type=F32
                )
                stage[j] = (res * factor).astype(BF16)
                cols = pl.ds(pl.multiple_of(table[entries[j]] * rows, rows), rows)
                copy = pltpu.make_async_copy(stage.at[j], out.at[:, cols], sems.at[j])
                copy.start()
                copies.append(copy)
        for copy in copies:
            copy.wait()

    return pl.pallas_call(
        body,
        out_shape=jax.ShapeDtypeStruct((cotan.shape[0], width), BF16),
        in_specs=specs,
        out_specs=ANY_SPEC,
        scratch_shapes=[
            pltpu.VMEM((total, cotan.shape[0], rows), BF16),
            pltpu.SemaphoreType.DMA((total,)),
        ],
        input_output_aliases=aliases,
        compiler_params=params(),
        cost_estimate=COST,
    )(*operands)


def mix_start(place, slope, islands, master, outer, momentum):
    rows, kvw = master.shape
    share, head = outer.shape

    def body(place, master, outer, momentum, out):
        turned = pltpu.roll(master[...], kvw - place[0], 1)
        out[...] = (slope / islands) * turned[:, :head]
        fixed = (1.0 - slope) * outer[...] - OUTER_RATE * MOMENTUM * MOMENTUM * momentum[...]
        own = pl.ds(pl.multiple_of(place[1], share), share)
        out[own, :] = out[own, :] + fixed

    return pl.pallas_call(
        body,
        out_shape=jax.ShapeDtypeStruct((rows, head), F32),
        in_specs=[SMEM_SPEC] + [VMEM_SPEC] * 3,
        out_specs=VMEM_SPEC,
        compiler_params=params(),
        cost_estimate=COST,
    )(place, master, outer, momentum)


def inner_step(place, slope, own, one, two, master, first, second, mix, outer, momentum):
    rows, kvw = master.shape
    share, head = outer.shape

    def body(place, own, one, two, master, first, second, mix, outer, momentum, *outs):
        w_out, f_out, s_out, o_out, m_out = outs
        gradient = (own[...].astype(F32) + (one[...].astype(F32) + two[...].astype(F32))).T
        weights = master[...]
        moment_one = BETA_FIRST * first[...] + (1.0 - BETA_FIRST) * gradient
        moment_two = BETA_SECOND * second[...] + (1.0 - BETA_SECOND) * gradient * gradient
        f_out[...] = moment_one
        s_out[...] = moment_two
        stepped = weights - INNER_RATE * (
            moment_one / (jnp.sqrt(moment_two) + EPSILON) + DECAY_RATE * weights
        )
        column = lax.broadcasted_iota(jnp.int32, stepped.shape, 1)
        inside = (column >= place[0]) & (column < place[0] + head)
        padding = jnp.zeros((rows, kvw - head), F32)
        placed = pltpu.roll(jnp.concatenate([mix[...], padding], axis=1), place[0], 1)
        w_out[...] = jnp.where(
            inside, MIX_WEIGHT * stepped + (1.0 - MIX_WEIGHT) * placed, stepped
        )
        fixed = (1.0 - slope) * outer[...] - OUTER_RATE * MOMENTUM * MOMENTUM * momentum[...]
        outer_next = mix[pl.ds(pl.multiple_of(place[1], share), share), :]
        o_out[...] = outer_next
        m_out[...] = MOMENTUM * momentum[...] + (outer[...] - (outer_next - fixed) / slope)

    return pl.pallas_call(
        body,
        out_shape=[jax.ShapeDtypeStruct(master.shape, F32)] * 3
        + [jax.ShapeDtypeStruct(outer.shape, F32)] * 2,
        in_specs=[SMEM_SPEC] + [VMEM_SPEC] * 9,
        out_specs=[VMEM_SPEC] * 5,
        compiler_params=params(),
        cost_estimate=COST,
    )(place, own, one, two, master, first, second, mix, outer, momentum)


def local(
    normed, cotangent, weights, first_moment, second_moment, outer_params, outer_momentum, fragment
):
    tokens_in, cotan, master = normed[0], cotangent[0], weights[0]
    rows, kvw = master.shape
    width = tokens_in.shape[1]
    factor = 1.0 / math.sqrt(width)
    me = lax.axis_index("fsdp")
    z, y, c = me // (NY * NC), (me // NC) % NY, me % NC

    def send(value, pairs, name):
        with jax.named_scope(name):
            return lax.ppermute(value, "fsdp", pairs)

    def send_island(value, pairs, name):
        with jax.named_scope(name):
            return lax.ppermute(value, "island", pairs)

    blocks = []
    for core, turn in ((c, 1 - 2 * c), (1 - c, 2 * c - 1)):
        for t in range(NY):
            for s in range(NZ):
                bz, by = (z - s * turn + NZ) % NZ, (y - t * turn + NY) % NY
                blocks.append((bz * NY + by) * NC + core)
    table = jnp.stack(blocks).astype(jnp.int32)

    def entry(core, t, s):
        return (core * NY + t % NY) * NZ + s % NZ

    def tie(*values):
        nonlocal table
        table, *tied = lax.optimization_barrier((table, *values))
        return tied[0] if len(tied) == 1 else tied

    islands = lax.axis_size("island")
    slope = OUTER_RATE * (1.0 + MOMENTUM)
    row_start = lax.axis_index("island") * outer_params.shape[0]
    place = jnp.stack([fragment[0], row_start.astype(jnp.int32)])

    order = (2, 1, 3, 0)
    first_places = [(2, s) for s in order]
    late_places = [(t, s) for t in (1, 3, 0) for s in order]

    def entries(core, places):
        return [entry(core, t, s) for t, s in places]

    swapping, swapping_late, own = tie(
        *pack(
            table,
            [
                entries(1, first_places),
                entries(1, late_places),
                entries(0, first_places + late_places),
            ],
            tokens_in,
            cotan,
            rows,
        )
    )
    swapped = send(swapping, SWAP, "swap_inputs")
    swapped_late = send(swapping_late, SWAP, "swap_inputs_late")
    w_half = tie(halve(tie(master)))
    za = send(w_half, ON_Z, "z_on")
    zb = send(w_half, BACK_Z, "z_back")

    swapped = tie(swapped)
    first = tie(*grad_blocks(0, 0, 1, factor, own, swapped, swapped))
    far = send(first, ON_Y, "r_far")
    swapped_late = tie(swapped_late)
    first, part_on, part_own = tie(
        *grad_blocks(NZ, 0, 3, factor, own, swapped, swapped_late)
    )
    near_back = send(first, BACK_Y, "r_back")

    mix = tie(mix_start(place, slope, islands, master, outer_params, outer_momentum))
    mix_x = send_island(mix.astype(BF16), SWAP_H, "frag_h")
    za = tie(za)
    zc = send(za, ON_Z, "z_far")
    zb = tie(zb)
    mix_x = tie(mix_x)
    mix = tie(mix + mix_x.astype(F32))
    mix_x = send_island(mix, PAIR_X, "frag_x1")
    far, near_back = tie(far, near_back)
    near_on = send(tie(*add(part_on, far)), ON_Y, "r_on")
    zc = tie(zc)
    near = tie(join([w_half, za, zb, zc]))
    z_order = (0, 1, 3, 2)
    swap_near = send(near, SWAP, "swap_near")
    ga = send(near, ON_Y, "g_on")
    gb = send(near, BACK_Y, "g_back")
    mix_x = tie(mix_x)
    mix = tie(mix + mix_x)
    mix_x = send_island(mix, CROSS_X, "frag_x2")
    mix_x = tie(mix_x)
    mix = tie(mix + mix_x)

    def batch(groups, back):
        pieces, places = [], []
        for piece, swapped, t in groups:
            pieces += [piece, swapped]
            places += [entry(core, t, s) for core in (0, 1) for s in z_order]
        return tie(input_blocks(table, places, cotan, pieces, width, factor, back))

    near_on = tie(near_on)
    z_far, z_back, z_on, z_own = tie(*add(part_own, near_back, near_on, split=True))
    far = send(z_far, ON_Z, "rz_far")
    near_back = send(z_back, BACK_Z, "rz_back")
    swap_near = tie(swap_near)
    back = batch([(near, swap_near, 0)], None)
    far = tie(far)
    near_on = send(tie(add_one(z_on, far)), ON_Z, "rz_on")
    ga = tie(ga)
    gc = send(ga, ON_Y, "g_far")
    swap_1 = send(ga, SWAP, "swap_on")
    gb = tie(gb)
    swap_3 = send(gb, SWAP, "swap_back")
    swap_1, swap_3 = tie(swap_1, swap_3)
    back = batch([(ga, swap_1, 1), (gb, swap_3, 3)], back)
    near_back, near_on = tie(near_back, near_on)
    gc = tie(gc)
    swap_2 = send(gc, SWAP, "swap_far")
    merged, moment_one, moment_two, outer_next, momentum_next = tie(
        *inner_step(
            place,
            slope,
            z_own,
            near_back,
            near_on,
            master,
            first_moment[0],
            second_moment[0],
            mix,
            outer_params,
            outer_momentum,
        )
    )
    swap_2 = tie(swap_2)
    back = batch([(gc, swap_2, 2)], back)
    return (
        back[None],
        merged[None],
        moment_one[None],
        moment_two[None],
        outer_next,
        momentum_next,
    )


def solution(mesh):
    return jax.shard_map(
        local,
        mesh=mesh,
        in_specs=(
            P("island", "fsdp", None),
            P("island", "fsdp", None),
            P("island", "fsdp", None),
            P("island", "fsdp", None),
            P("island", "fsdp", None),
            P(("fsdp", "island"), None),
            P(("fsdp", "island"), None),
            P(),
        ),
        out_specs=(
            P("island", "fsdp", None),
            P("island", "fsdp", None),
            P("island", "fsdp", None),
            P("island", "fsdp", None),
            P(("fsdp", "island"), None),
            P(("fsdp", "island"), None),
        ),
        check_vma=False,
    )
```

```python
import math

import jax
import jax.numpy as jnp
from jax import lax
from jax.experimental import pallas as pl
from jax.experimental.pallas import tpu as pltpu
from jax.sharding import PartitionSpec as P

BETA_FIRST = 0.9
BETA_SECOND = 0.95
EPSILON = 1e-08
INNER_RATE = 0.01
DECAY_RATE = 0.1
OUTER_RATE = 0.7
MOMENTUM = 0.9
MIX_WEIGHT = 0.5

NZ, NY, NC = 4, 4, 2
NX = 4
F32, BF16 = jnp.float32, jnp.bfloat16
COST = pl.CostEstimate(flops=1, bytes_accessed=1, transcendentals=0)
VMEM_LIMIT = 8 * 1024 * 1024

SMEM_SPEC = pl.BlockSpec(memory_space=pltpu.SMEM)
VMEM_SPEC = pl.BlockSpec(memory_space=pltpu.VMEM)
ANY_SPEC = pl.BlockSpec(memory_space=pl.ANY)


def fsdp_perm(move):
    pairs = []
    for z in range(NZ):
        for y in range(NY):
            for c in range(NC):
                tz, ty, tc = move(z, y, c)
                pairs.append(((z * NY + y) * NC + c, ((tz % NZ) * NY + ty % NY) * NC + tc))
    return pairs


def turned_perms(move):
    return [fsdp_perm(lambda z, y, c, k=k: move(z, y, c, k if c == 0 else -k)) for k in (1, -1)]


ON_Y, BACK_Y = turned_perms(lambda z, y, c, k: (z, y + k, c))
ON_Z, BACK_Z = turned_perms(lambda z, y, c, k: (z + k, y, c))
SWAP = fsdp_perm(lambda z, y, c: (z, y, 1 - c))


def island_perm(move):
    pairs = []
    for h in range(2):
        for x in range(NX):
            th, tx = move(h, x)
            pairs.append((h * NX + x, th * NX + tx))
    return pairs


PAIR_X = island_perm(lambda h, x: (h, x ^ 1))
CROSS_X = island_perm(lambda h, x: (h, 3 - x))
SWAP_H = island_perm(lambda h, x: (1 - h, x))


def params():
    return pltpu.CompilerParams(vmem_limit_bytes=VMEM_LIMIT)


def halve(master):
    def body(master, out):
        out[...] = master[...].astype(BF16)

    return pl.pallas_call(
        body,
        out_shape=jax.ShapeDtypeStruct(master.shape, BF16),
        in_specs=[VMEM_SPEC],
        out_specs=VMEM_SPEC,
        compiler_params=params(),
        cost_estimate=COST,
    )(master)


def pack(table, groups, normed, cotan, rows):
    tokens, kvw = cotan.shape
    halves = kvw // rows
    extra = [halves] + [0] * (len(groups) - 2) + [halves]

    def body(table, normed, cotan, *outs):
        for h in range(halves):
            turned = cotan[:, h * rows : (h + 1) * rows].T
            for i in (0, len(groups) - 1):
                outs[i][len(groups[i]) + h] = turned
        for out, places in zip(outs, groups):
            for j, place in enumerate(places):
                cols = pl.ds(pl.multiple_of(table[place] * rows, rows), rows)
                out[j] = normed[:, cols]

    return pl.pallas_call(
        body,
        out_shape=[
            jax.ShapeDtypeStruct((len(g) + n, tokens, rows), BF16) for g, n in zip(groups, extra)
        ],
        in_specs=[SMEM_SPEC] + [VMEM_SPEC] * 2,
        out_specs=[VMEM_SPEC] * len(groups),
        compiler_params=params(),
        cost_estimate=COST,
    )(table, normed, cotan)


def join(pieces):
    def body(*refs):
        at = 0
        for ref in refs[:-1]:
            refs[-1][pl.ds(at, ref.shape[0]), :] = ref[...]
            at += ref.shape[0]

    rows, columns = pieces[0].shape
    return pl.pallas_call(
        body,
        out_shape=jax.ShapeDtypeStruct((len(pieces) * rows, columns), pieces[0].dtype),
        in_specs=[VMEM_SPEC] * len(pieces),
        out_specs=VMEM_SPEC,
        compiler_params=params(),
        cost_estimate=COST,
    )(*pieces)


def grad_blocks(first, packed_first, groups, factor, own, swapped, packed):
    width = own.shape[2]
    halves = 2

    def body(own, swapped, packed, *outs):
        for group, out in enumerate(outs):
            for j in range(NZ):
                at = group * NZ + j
                for half in range(halves):
                    mine, theirs = own.shape[0] - halves + half, swapped.shape[0] - halves + half
                    total = jnp.dot(own[mine], own[first + at], preferred_element_type=F32)
                    total += jnp.dot(
                        swapped[theirs], packed[packed_first + at], preferred_element_type=F32
                    )
                    out[j, pl.ds(half * width, width), :] = (total * factor).astype(BF16)

    return pl.pallas_call(
        body,
        out_shape=[jax.ShapeDtypeStruct((NZ, halves * width, width), BF16)] * groups,
        in_specs=[VMEM_SPEC] * 3,
        out_specs=[VMEM_SPEC] * groups,
        compiler_params=params(),
        cost_estimate=COST,
    )(own, swapped, packed)


def add(*parts, split=False):
    blocks, *block = parts[0].shape

    def body(*refs):
        ins, outs = refs[: len(parts)], refs[len(parts) :]
        for j in range(blocks):
            total = ins[0][j].astype(F32)
            for ref in ins[1:]:
                total += ref[j].astype(F32)
            if split:
                outs[j][...] = total.astype(BF16)
            else:
                outs[0][j] = total.astype(BF16)

    shapes = [block] * blocks if split else [parts[0].shape]
    return pl.pallas_call(
        body,
        out_shape=[jax.ShapeDtypeStruct(tuple(shape), BF16) for shape in shapes],
        in_specs=[VMEM_SPEC] * len(parts),
        out_specs=[VMEM_SPEC] * len(shapes),
        compiler_params=params(),
        cost_estimate=COST,
    )(*parts)


def add_one(a, b):
    def body(a, b, out):
        out[...] = (a[...].astype(F32) + b[...].astype(F32)).astype(BF16)

    return pl.pallas_call(
        body,
        out_shape=jax.ShapeDtypeStruct(a.shape, BF16),
        in_specs=[VMEM_SPEC] * 2,
        out_specs=VMEM_SPEC,
        compiler_params=params(),
        cost_estimate=COST,
    )(a, b)


def input_blocks(table, entries, cotan, pieces, width, factor, dest=None):
    rows = width // (NZ * NY * NC)
    total = len(entries)
    operands = [table, cotan, *pieces]
    specs = [SMEM_SPEC] + [VMEM_SPEC] * (1 + len(pieces))
    aliases = {}
    if dest is not None:
        aliases = {len(operands): 0}
        operands.append(dest)
        specs.append(ANY_SPEC)

    def body(table, cotan, *refs):
        out, stage, sems = refs[-3:]
        copies = []
        for piece in refs[: len(pieces)]:
            for b in range(piece.shape[0] // rows):
                j = len(copies)
                block = piece[pl.ds(b * rows, rows), :]
                res = lax.dot_general(
                    cotan[...], block, (((1,), (1,)), ((), ())), preferred_element_type=F32
                )
                stage[j] = (res * factor).astype(BF16)
                cols = pl.ds(pl.multiple_of(table[entries[j]] * rows, rows), rows)
                copy = pltpu.make_async_copy(stage.at[j], out.at[:, cols], sems.at[j])
                copy.start()
                copies.append(copy)
        for copy in copies:
            copy.wait()

    return pl.pallas_call(
        body,
        out_shape=jax.ShapeDtypeStruct((cotan.shape[0], width), BF16),
        in_specs=specs,
        out_specs=ANY_SPEC,
        scratch_shapes=[
            pltpu.VMEM((total, cotan.shape[0], rows), BF16),
            pltpu.SemaphoreType.DMA((total,)),
        ],
        input_output_aliases=aliases,
        compiler_params=params(),
        cost_estimate=COST,
    )(*operands)


def mix_start(place, slope, islands, master, outer, momentum):
    rows, kvw = master.shape
    share, head = outer.shape

    def body(place, master, outer, momentum, out):
        turned = pltpu.roll(master[...], kvw - place[0], 1)
        out[...] = (slope / islands) * turned[:, :head]
        fixed = (1.0 - slope) * outer[...] - OUTER_RATE * MOMENTUM * MOMENTUM * momentum[...]
        own = pl.ds(pl.multiple_of(place[1], share), share)
        out[own, :] = out[own, :] + fixed

    return pl.pallas_call(
        body,
        out_shape=jax.ShapeDtypeStruct((rows, head), F32),
        in_specs=[SMEM_SPEC] + [VMEM_SPEC] * 3,
        out_specs=VMEM_SPEC,
        compiler_params=params(),
        cost_estimate=COST,
    )(place, master, outer, momentum)


def inner_step(place, slope, own, one, two, master, first, second, mix, outer, momentum):
    rows, kvw = master.shape
    share, head = outer.shape

    def body(place, own, one, two, master, first, second, mix, outer, momentum, *outs):
        w_out, f_out, s_out, o_out, m_out = outs
        gradient = (own[...].astype(F32) + (one[...].astype(F32) + two[...].astype(F32))).T
        weights = master[...]
        moment_one = BETA_FIRST * first[...] + (1.0 - BETA_FIRST) * gradient
        moment_two = BETA_SECOND * second[...] + (1.0 - BETA_SECOND) * gradient * gradient
        f_out[...] = moment_one
        s_out[...] = moment_two
        stepped = weights - INNER_RATE * (
            moment_one / (jnp.sqrt(moment_two) + EPSILON) + DECAY_RATE * weights
        )
        column = lax.broadcasted_iota(jnp.int32, stepped.shape, 1)
        inside = (column >= place[0]) & (column < place[0] + head)
        padding = jnp.zeros((rows, kvw - head), F32)
        placed = pltpu.roll(jnp.concatenate([mix[...], padding], axis=1), place[0], 1)
        w_out[...] = jnp.where(
            inside, MIX_WEIGHT * stepped + (1.0 - MIX_WEIGHT) * placed, stepped
        )
        fixed = (1.0 - slope) * outer[...] - OUTER_RATE * MOMENTUM * MOMENTUM * momentum[...]
        outer_next = mix[pl.ds(pl.multiple_of(place[1], share), share), :]
        o_out[...] = outer_next
        m_out[...] = MOMENTUM * momentum[...] + (outer[...] - (outer_next - fixed) / slope)

    return pl.pallas_call(
        body,
        out_shape=[jax.ShapeDtypeStruct(master.shape, F32)] * 3
        + [jax.ShapeDtypeStruct(outer.shape, F32)] * 2,
        in_specs=[SMEM_SPEC] + [VMEM_SPEC] * 9,
        out_specs=[VMEM_SPEC] * 5,
        compiler_params=params(),
        cost_estimate=COST,
    )(place, own, one, two, master, first, second, mix, outer, momentum)


def local(
    normed, cotangent, weights, first_moment, second_moment, outer_params, outer_momentum, fragment
):
    tokens_in, cotan, master = normed[0], cotangent[0], weights[0]
    rows, kvw = master.shape
    width = tokens_in.shape[1]
    factor = 1.0 / math.sqrt(width)
    me = lax.axis_index("fsdp")
    z, y, c = me // (NY * NC), (me // NC) % NY, me % NC

    def send(value, pairs, name):
        with jax.named_scope(name):
            return lax.ppermute(value, "fsdp", pairs)

    def send_island(value, pairs, name):
        with jax.named_scope(name):
            return lax.ppermute(value, "island", pairs)

    blocks = []
    for core, turn in ((c, 1 - 2 * c), (1 - c, 2 * c - 1)):
        for t in range(NY):
            for s in range(NZ):
                bz, by = (z - s * turn + NZ) % NZ, (y - t * turn + NY) % NY
                blocks.append((bz * NY + by) * NC + core)
    table = jnp.stack(blocks).astype(jnp.int32)

    def entry(core, t, s):
        return (core * NY + t % NY) * NZ + s % NZ

    def tie(*values):
        nonlocal table
        table, *tied = lax.optimization_barrier((table, *values))
        return tied[0] if len(tied) == 1 else tied

    islands = lax.axis_size("island")
    slope = OUTER_RATE * (1.0 + MOMENTUM)
    row_start = lax.axis_index("island") * outer_params.shape[0]
    place = jnp.stack([fragment[0], row_start.astype(jnp.int32)])

    order = (2, 1, 3, 0)
    first_places = [(2, s) for s in order]
    late_places = [(t, s) for t in (1, 3, 0) for s in order]

    def entries(core, places):
        return [entry(core, t, s) for t, s in places]

    swapping, swapping_late, own = tie(
        *pack(
            table,
            [
                entries(1, first_places),
                entries(1, late_places),
                entries(0, first_places + late_places),
            ],
            tokens_in,
            cotan,
            rows,
        )
    )
    swapped = tie(send(swapping, SWAP, "swap_inputs"))
    swapped_late = send(tie(swapping_late), SWAP, "swap_inputs_late")
    first = tie(*grad_blocks(0, 0, 1, factor, own, swapped, swapped))
    far = send(first, ON_Y, "r_far")
    swapped_late = tie(swapped_late)
    first, part_on, part_own = tie(*grad_blocks(NZ, 0, 3, factor, own, swapped, swapped_late))
    near_back = send(first, BACK_Y, "r_back")
    w_half = tie(halve(tie(master)))
    za = send(w_half, ON_Z, "z_on")
    zb = send(w_half, BACK_Z, "z_back")
    za = tie(za)
    zc = send(za, ON_Z, "z_far")
    zb = tie(zb)
    far = tie(far)
    near_on = send(tie(*add(part_on, far)), ON_Y, "r_on")
    zc = tie(zc)
    near = tie(join([w_half, za, zb, zc]))
    z_order = (0, 1, 3, 2)
    swap_near = send(near, SWAP, "swap_near")
    ga = send(near, ON_Y, "g_on")
    gb = send(near, BACK_Y, "g_back")
    near_back = tie(near_back)
    part_own = tie(*add(part_own, near_back))

    mix = tie(mix_start(place, slope, islands, tie(master), outer_params, outer_momentum))
    mix_x = send_island(mix.astype(BF16), SWAP_H, "frag_h")
    mix_x = tie(mix_x)
    mix = tie(mix + mix_x.astype(F32))
    mix_x = send_island(mix, PAIR_X, "frag_x1")
    mix_x = tie(mix_x)
    mix = tie(mix + mix_x)
    mix_x = send_island(mix, CROSS_X, "frag_x2")

    def batch(groups, back):
        pieces, places = [], []
        for piece, swapped, t in groups:
            pieces += [piece, swapped]
            places += [entry(core, t, s) for core in (0, 1) for s in z_order]
        return tie(input_blocks(table, places, cotan, pieces, width, factor, back))

    near_on = tie(near_on)
    z_far, z_back, z_on, z_own = tie(*add(part_own, near_on, split=True))
    far = send(z_far, ON_Z, "rz_far")
    swap_near = tie(swap_near)
    near_back = send(z_back, BACK_Z, "rz_back")
    mix_x = tie(mix_x)
    mix = tie(mix + mix_x)
    far = tie(far)
    near_on = send(tie(add_one(z_on, far)), ON_Z, "rz_on")
    ga, gb = tie(ga, gb)
    gc = send(ga, ON_Y, "g_far")
    swap_1 = send(ga, SWAP, "swap_on")
    swap_3 = send(gb, SWAP, "swap_back")
    swap_1, swap_3 = tie(swap_1, swap_3)
    back = batch([(ga, swap_1, 1), (gb, swap_3, 3)], None)
    back = batch([(near, swap_near, 0)], back)
    near_back, near_on = tie(near_back, near_on)
    gc = tie(gc)
    swap_2 = send(gc, SWAP, "swap_far")
    merged, moment_one, moment_two, outer_next, momentum_next = tie(
        *inner_step(
            place,
            slope,
            z_own,
            near_back,
            near_on,
            master,
            first_moment[0],
            second_moment[0],
            mix,
            outer_params,
            outer_momentum,
        )
    )
    swap_2 = tie(swap_2)
    back = batch([(gc, swap_2, 2)], back)
    return (
        back[None],
        merged[None],
        moment_one[None],
        moment_two[None],
        outer_next,
        momentum_next,
    )


def solution(mesh):
    return jax.shard_map(
        local,
        mesh=mesh,
        in_specs=(
            P("island", "fsdp", None),
            P("island", "fsdp", None),
            P("island", "fsdp", None),
            P("island", "fsdp", None),
            P("island", "fsdp", None),
            P(("fsdp", "island"), None),
            P(("fsdp", "island"), None),
            P(),
        ),
        out_specs=(
            P("island", "fsdp", None),
            P("island", "fsdp", None),
            P("island", "fsdp", None),
            P("island", "fsdp", None),
            P(("fsdp", "island"), None),
            P(("fsdp", "island"), None),
        ),
        check_vma=False,
    )
```

```python
import math

import jax
import jax.numpy as jnp
from jax import lax
from jax.experimental import pallas as pl
from jax.experimental.pallas import tpu as pltpu
from jax.sharding import PartitionSpec as P

BETA_FIRST = 0.9
BETA_SECOND = 0.95
EPSILON = 1e-08
INNER_RATE = 0.01
DECAY_RATE = 0.1
OUTER_RATE = 0.7
MOMENTUM = 0.9
MIX_WEIGHT = 0.5

NZ, NY, NC = 4, 4, 2
NX = 4
F32, BF16 = jnp.float32, jnp.bfloat16
COST = pl.CostEstimate(flops=1, bytes_accessed=1, transcendentals=0)
VMEM_LIMIT = 8 * 1024 * 1024

SMEM_SPEC = pl.BlockSpec(memory_space=pltpu.SMEM)
VMEM_SPEC = pl.BlockSpec(memory_space=pltpu.VMEM)
ANY_SPEC = pl.BlockSpec(memory_space=pl.ANY)


def fsdp_perm(move):
    pairs = []
    for z in range(NZ):
        for y in range(NY):
            for c in range(NC):
                tz, ty, tc = move(z, y, c)
                pairs.append(((z * NY + y) * NC + c, ((tz % NZ) * NY + ty % NY) * NC + tc))
    return pairs


def turned_perms(move):
    return [fsdp_perm(lambda z, y, c, k=k: move(z, y, c, k if c == 0 else -k)) for k in (1, -1)]


ON_Y, BACK_Y = turned_perms(lambda z, y, c, k: (z, y + k, c))
ON_Z, BACK_Z = turned_perms(lambda z, y, c, k: (z + k, y, c))
SWAP = fsdp_perm(lambda z, y, c: (z, y, 1 - c))


def island_perm(move):
    pairs = []
    for h in range(2):
        for x in range(NX):
            th, tx = move(h, x)
            pairs.append((h * NX + x, th * NX + tx))
    return pairs


PAIR_X = island_perm(lambda h, x: (h, x ^ 1))
CROSS_X = island_perm(lambda h, x: (h, 3 - x))
SWAP_H = island_perm(lambda h, x: (1 - h, x))


def params():
    return pltpu.CompilerParams(vmem_limit_bytes=VMEM_LIMIT)


def halve(master):
    def body(master, out):
        out[...] = master[...].astype(BF16)

    return pl.pallas_call(
        body,
        out_shape=jax.ShapeDtypeStruct(master.shape, BF16),
        in_specs=[VMEM_SPEC],
        out_specs=VMEM_SPEC,
        compiler_params=params(),
        cost_estimate=COST,
    )(master)


def pack(table, groups, normed, cotan, rows):
    tokens, kvw = cotan.shape
    halves = kvw // rows
    extra = [halves] + [0] * (len(groups) - 2) + [halves]

    def body(table, normed, cotan, *outs):
        for h in range(halves):
            turned = cotan[:, h * rows : (h + 1) * rows].T
            for i in (0, len(groups) - 1):
                outs[i][len(groups[i]) + h] = turned
        for out, places in zip(outs, groups):
            for j, place in enumerate(places):
                cols = pl.ds(pl.multiple_of(table[place] * rows, rows), rows)
                out[j] = normed[:, cols]

    return pl.pallas_call(
        body,
        out_shape=[
            jax.ShapeDtypeStruct((len(g) + n, tokens, rows), BF16) for g, n in zip(groups, extra)
        ],
        in_specs=[SMEM_SPEC] + [VMEM_SPEC] * 2,
        out_specs=[VMEM_SPEC] * len(groups),
        compiler_params=params(),
        cost_estimate=COST,
    )(table, normed, cotan)


def join(pieces):
    def body(*refs):
        at = 0
        for ref in refs[:-1]:
            refs[-1][pl.ds(at, ref.shape[0]), :] = ref[...]
            at += ref.shape[0]

    rows, columns = pieces[0].shape
    return pl.pallas_call(
        body,
        out_shape=jax.ShapeDtypeStruct((len(pieces) * rows, columns), pieces[0].dtype),
        in_specs=[VMEM_SPEC] * len(pieces),
        out_specs=VMEM_SPEC,
        compiler_params=params(),
        cost_estimate=COST,
    )(*pieces)


def grad_blocks(first, packed_first, groups, factor, own, swapped, packed):
    width = own.shape[2]
    halves = 2

    def body(own, swapped, packed, *outs):
        for group, out in enumerate(outs):
            for j in range(NZ):
                at = group * NZ + j
                for half in range(halves):
                    mine, theirs = own.shape[0] - halves + half, swapped.shape[0] - halves + half
                    total = jnp.dot(own[mine], own[first + at], preferred_element_type=F32)
                    total += jnp.dot(
                        swapped[theirs], packed[packed_first + at], preferred_element_type=F32
                    )
                    out[j, pl.ds(half * width, width), :] = (total * factor).astype(BF16)

    return pl.pallas_call(
        body,
        out_shape=[jax.ShapeDtypeStruct((NZ, halves * width, width), BF16)] * groups,
        in_specs=[VMEM_SPEC] * 3,
        out_specs=[VMEM_SPEC] * groups,
        compiler_params=params(),
        cost_estimate=COST,
    )(own, swapped, packed)


def add(*parts, split=False):
    blocks, *block = parts[0].shape

    def body(*refs):
        ins, outs = refs[: len(parts)], refs[len(parts) :]
        for j in range(blocks):
            total = ins[0][j].astype(F32)
            for ref in ins[1:]:
                total += ref[j].astype(F32)
            if split:
                outs[j][...] = total.astype(BF16)
            else:
                outs[0][j] = total.astype(BF16)

    shapes = [block] * blocks if split else [parts[0].shape]
    return pl.pallas_call(
        body,
        out_shape=[jax.ShapeDtypeStruct(tuple(shape), BF16) for shape in shapes],
        in_specs=[VMEM_SPEC] * len(parts),
        out_specs=[VMEM_SPEC] * len(shapes),
        compiler_params=params(),
        cost_estimate=COST,
    )(*parts)


def add_one(a, b):
    def body(a, b, out):
        out[...] = (a[...].astype(F32) + b[...].astype(F32)).astype(BF16)

    return pl.pallas_call(
        body,
        out_shape=jax.ShapeDtypeStruct(a.shape, BF16),
        in_specs=[VMEM_SPEC] * 2,
        out_specs=VMEM_SPEC,
        compiler_params=params(),
        cost_estimate=COST,
    )(a, b)


def input_blocks(table, entries, cotan, pieces, width, factor, dest=None):
    rows = width // (NZ * NY * NC)
    total = len(entries)
    operands = [table, cotan, *pieces]
    specs = [SMEM_SPEC] + [VMEM_SPEC] * (1 + len(pieces))
    aliases = {}
    if dest is not None:
        aliases = {len(operands): 0}
        operands.append(dest)
        specs.append(ANY_SPEC)

    def body(table, cotan, *refs):
        out, stage, sems = refs[-3:]
        copies = []
        for piece in refs[: len(pieces)]:
            for b in range(piece.shape[0] // rows):
                j = len(copies)
                block = piece[pl.ds(b * rows, rows), :]
                res = lax.dot_general(
                    cotan[...], block, (((1,), (1,)), ((), ())), preferred_element_type=F32
                )
                stage[j] = (res * factor).astype(BF16)
                cols = pl.ds(pl.multiple_of(table[entries[j]] * rows, rows), rows)
                copy = pltpu.make_async_copy(stage.at[j], out.at[:, cols], sems.at[j])
                copy.start()
                copies.append(copy)
        for copy in copies:
            copy.wait()

    return pl.pallas_call(
        body,
        out_shape=jax.ShapeDtypeStruct((cotan.shape[0], width), BF16),
        in_specs=specs,
        out_specs=ANY_SPEC,
        scratch_shapes=[
            pltpu.VMEM((total, cotan.shape[0], rows), BF16),
            pltpu.SemaphoreType.DMA((total,)),
        ],
        input_output_aliases=aliases,
        compiler_params=params(),
        cost_estimate=COST,
    )(*operands)


def mix_start(place, slope, islands, master, outer, momentum):
    rows, kvw = master.shape
    share, head = outer.shape

    def body(place, master, outer, momentum, out):
        turned = pltpu.roll(master[...], kvw - place[0], 1)
        out[...] = (slope / islands) * turned[:, :head]
        fixed = (1.0 - slope) * outer[...] - OUTER_RATE * MOMENTUM * MOMENTUM * momentum[...]
        own = pl.ds(pl.multiple_of(place[1], share), share)
        out[own, :] = out[own, :] + fixed

    return pl.pallas_call(
        body,
        out_shape=jax.ShapeDtypeStruct((rows, head), F32),
        in_specs=[SMEM_SPEC] + [VMEM_SPEC] * 3,
        out_specs=VMEM_SPEC,
        compiler_params=params(),
        cost_estimate=COST,
    )(place, master, outer, momentum)


def inner_step(place, slope, own, one, two, master, first, second, mix, outer, momentum):
    rows, kvw = master.shape
    share, head = outer.shape

    def body(place, own, one, two, master, first, second, mix, outer, momentum, *outs):
        w_out, f_out, s_out, o_out, m_out = outs
        gradient = (own[...].astype(F32) + (one[...].astype(F32) + two[...].astype(F32))).T
        weights = master[...]
        moment_one = BETA_FIRST * first[...] + (1.0 - BETA_FIRST) * gradient
        moment_two = BETA_SECOND * second[...] + (1.0 - BETA_SECOND) * gradient * gradient
        f_out[...] = moment_one
        s_out[...] = moment_two
        stepped = weights - INNER_RATE * (
            moment_one / (jnp.sqrt(moment_two) + EPSILON) + DECAY_RATE * weights
        )
        column = lax.broadcasted_iota(jnp.int32, stepped.shape, 1)
        inside = (column >= place[0]) & (column < place[0] + head)
        padding = jnp.zeros((rows, kvw - head), F32)
        placed = pltpu.roll(jnp.concatenate([mix[...], padding], axis=1), place[0], 1)
        w_out[...] = jnp.where(
            inside, MIX_WEIGHT * stepped + (1.0 - MIX_WEIGHT) * placed, stepped
        )
        fixed = (1.0 - slope) * outer[...] - OUTER_RATE * MOMENTUM * MOMENTUM * momentum[...]
        outer_next = mix[pl.ds(pl.multiple_of(place[1], share), share), :]
        o_out[...] = outer_next
        m_out[...] = MOMENTUM * momentum[...] + (outer[...] - (outer_next - fixed) / slope)

    return pl.pallas_call(
        body,
        out_shape=[jax.ShapeDtypeStruct(master.shape, F32)] * 3
        + [jax.ShapeDtypeStruct(outer.shape, F32)] * 2,
        in_specs=[SMEM_SPEC] + [VMEM_SPEC] * 9,
        out_specs=[VMEM_SPEC] * 5,
        compiler_params=params(),
        cost_estimate=COST,
    )(place, own, one, two, master, first, second, mix, outer, momentum)


def local(
    normed, cotangent, weights, first_moment, second_moment, outer_params, outer_momentum, fragment
):
    tokens_in, cotan, master = normed[0], cotangent[0], weights[0]
    rows, kvw = master.shape
    width = tokens_in.shape[1]
    factor = 1.0 / math.sqrt(width)
    me = lax.axis_index("fsdp")
    z, y, c = me // (NY * NC), (me // NC) % NY, me % NC

    def send(value, pairs, name):
        with jax.named_scope(name):
            return lax.ppermute(value, "fsdp", pairs)

    def send_island(value, pairs, name):
        with jax.named_scope(name):
            return lax.ppermute(value, "island", pairs)

    blocks = []
    for core, turn in ((c, 1 - 2 * c), (1 - c, 2 * c - 1)):
        for t in range(NY):
            for s in range(NZ):
                bz, by = (z - s * turn + NZ) % NZ, (y - t * turn + NY) % NY
                blocks.append((bz * NY + by) * NC + core)
    table = jnp.stack(blocks).astype(jnp.int32)

    def entry(core, t, s):
        return (core * NY + t % NY) * NZ + s % NZ

    def tie(*values):
        nonlocal table
        table, *tied = lax.optimization_barrier((table, *values))
        return tied[0] if len(tied) == 1 else tied

    islands = lax.axis_size("island")
    slope = OUTER_RATE * (1.0 + MOMENTUM)
    row_start = lax.axis_index("island") * outer_params.shape[0]
    place = jnp.stack([fragment[0], row_start.astype(jnp.int32)])

    order = (2, 1, 3, 0)
    first_places = [(2, s) for s in order]
    late_places = [(t, s) for t in (1, 3, 0) for s in order]

    def entries(core, places):
        return [entry(core, t, s) for t, s in places]

    swapping, swapping_late, own = tie(
        *pack(
            table,
            [
                entries(1, first_places),
                entries(1, late_places),
                entries(0, first_places + late_places),
            ],
            tokens_in,
            cotan,
            rows,
        )
    )
    swapped = tie(send(swapping, SWAP, "swap_inputs"))
    swapped_late = send(tie(swapping_late), SWAP, "swap_inputs_late")
    first = tie(*grad_blocks(0, 0, 1, factor, own, swapped, swapped))
    far = send(first, ON_Y, "r_far")
    swapped_late = tie(swapped_late)
    first, part_on, part_own = tie(*grad_blocks(NZ, 0, 3, factor, own, swapped, swapped_late))
    near_back = send(first, BACK_Y, "r_back")
    w_half = tie(halve(tie(master)))
    za = send(w_half, ON_Z, "z_on")
    zb = send(w_half, BACK_Z, "z_back")
    za = tie(za)
    zc = send(za, ON_Z, "z_far")
    zb = tie(zb)
    far = tie(far)
    near_on = send(tie(*add(part_on, far)), ON_Y, "r_on")
    zc = tie(zc)
    near = tie(join([w_half, za, zb, zc]))
    z_order = (0, 1, 3, 2)
    swap_near = send(near, SWAP, "swap_near")
    ga = send(near, ON_Y, "g_on")
    gb = send(near, BACK_Y, "g_back")
    near_back = tie(near_back)

    mix = tie(mix_start(place, slope, islands, tie(master), outer_params, outer_momentum))
    mix_x = send_island(mix.astype(BF16), SWAP_H, "frag_h")
    mix_x = tie(mix_x)
    mix = tie(mix + mix_x.astype(F32))
    mix_x = send_island(mix, PAIR_X, "frag_x1")
    part_own = tie(*add(part_own, near_back))
    mix_x = tie(mix_x)
    mix = tie(mix + mix_x)
    mix_x = send_island(mix, CROSS_X, "frag_x2")

    def batch(groups, back):
        pieces, places = [], []
        for piece, swapped, t in groups:
            pieces += [piece, swapped]
            places += [entry(core, t, s) for core in (0, 1) for s in z_order]
        return tie(input_blocks(table, places, cotan, pieces, width, factor, back))

    near_on = tie(near_on)
    z_far, z_back, z_on, z_own = tie(*add(part_own, near_on, split=True))
    far = send(z_far, ON_Z, "rz_far")
    swap_near = tie(swap_near)
    near_back = send(z_back, BACK_Z, "rz_back")
    mix_x = tie(mix_x)
    mix = tie(mix + mix_x)
    far = tie(far)
    near_on = send(tie(add_one(z_on, far)), ON_Z, "rz_on")
    ga, gb = tie(ga, gb)
    gc = send(ga, ON_Y, "g_far")
    swap_1 = send(ga, SWAP, "swap_on")
    swap_3 = send(gb, SWAP, "swap_back")
    swap_1, swap_3 = tie(swap_1, swap_3)
    back = batch([(ga, swap_1, 1), (gb, swap_3, 3)], None)
    back = batch([(near, swap_near, 0)], back)
    near_back, near_on = tie(near_back, near_on)
    gc = tie(gc)
    swap_2 = send(gc, SWAP, "swap_far")
    merged, moment_one, moment_two, outer_next, momentum_next = tie(
        *inner_step(
            place,
            slope,
            z_own,
            near_back,
            near_on,
            master,
            first_moment[0],
            second_moment[0],
            mix,
            outer_params,
            outer_momentum,
        )
    )
    swap_2 = tie(swap_2)
    back = batch([(gc, swap_2, 2)], back)
    return (
        back[None],
        merged[None],
        moment_one[None],
        moment_two[None],
        outer_next,
        momentum_next,
    )


def solution(mesh):
    return jax.shard_map(
        local,
        mesh=mesh,
        in_specs=(
            P("island", "fsdp", None),
            P("island", "fsdp", None),
            P("island", "fsdp", None),
            P("island", "fsdp", None),
            P("island", "fsdp", None),
            P(("fsdp", "island"), None),
            P(("fsdp", "island"), None),
            P(),
        ),
        out_specs=(
            P("island", "fsdp", None),
            P("island", "fsdp", None),
            P("island", "fsdp", None),
            P("island", "fsdp", None),
            P(("fsdp", "island"), None),
            P(("fsdp", "island"), None),
        ),
        check_vma=False,
    )
```
